32 devices in a mesh: groups: 2 (over y), dp: 4 (over z), fsdp: 2 (over x), adapter: 2 (over core).
Axes of the slice: x: 2, y: 2, z: 4, core: 2. Of those that a mesh axis runs over, the one named last changes fastest.
Arguments:
- output_gradient: bfloat16 [3072, 8192], P(('groups', 'dp'), ('fsdp', 'adapter')), parts along dimension 0, may hold values from -4 to 4
- attention_output: bfloat16 [3072, 4096], P(('groups', 'dp'), ('fsdp', 'adapter')), parts along dimension 0, may hold values from -6 to 6
- frozen_weight: bfloat16 [4096, 8192], P(('fsdp', 'adapter'), 'dp'), may hold values from -0.0625 to 0.0625
- adapter_down_table: bfloat16 [256, 4096, 16], P(('groups', 'dp'), ('fsdp', 'adapter')), parts along dimension 0, may hold values from -1.5 to 1.5
- adapter_up_table: bfloat16 [256, 16, 8192], P(('groups', 'dp'), None, ('fsdp', 'adapter')), parts along dimension 0, may hold values from -0.0625 to 0.0625
- segment_adapter: int32 [16], P(('groups', 'dp')), parts along dimension 0, may hold values from 0 to 127, as said below
- segment_first_token: int32 [16], P(('groups', 'dp')), parts along dimension 0, may hold values from 0 to 383, as said below
- adapter_table_row: int32 [256], P('groups'), parts along dimension 0, may hold values from 0 to 127, as said below
Outputs:
- input_gradient: bfloat16 [3072, 4096], P(('groups', 'dp'), ('fsdp', 'adapter')), parts along dimension 0
- grad_a: bfloat16 [256, 4096, 16], P(('groups', 'dp'), ('fsdp', 'adapter')), parts along dimension 0
- grad_b: bfloat16 [256, 16, 8192], P(('groups', 'dp'), None, ('fsdp', 'adapter')), parts along dimension 0
The draws below stay inside these ranges and needn't reach their ends.
There are 2 independent parts, one for each index of `groups`. The reference program is written for one: setup_inputs(seed, part) draws one part's arguments, and reference() takes and returns one part's arrays. A program takes and returns all parts, laid end to end along the dimension named above; an argument that names none is the same for every part. Nothing has to cross between parts.
Inputs may be any that keep to these rules, and one draw needn't show every extreme that they name: `segment_adapter`: the 2 segments of one dp index name adapters whose table rows lie in the blocks of 32 rows of 2 different dp indices. `segment_first_token`: within each dp index, 2 increasing offsets with the first 0. `adapter_table_row`: a permutation of the table rows.
All inputs are finite; a program needn't handle non-finite values.
Results may differ from the reference program's by a relative error of at most 0.0049.
Values may be sent and summed in bfloat16 or wider, within the bound.
A program may use at most 128 MiB of HBM per device.

```python
import jax
import jax.numpy as jnp
from jax import lax

MODEL_WIDTH = 8192
ADAPTER_RANK = 16
ADP_DEV = 32
TOK_DP = 384
INPUT_FEATURES = 4096
ADAPTER_COUNT = 128
SEGS = 2
TOKENS = 1536
N_DP = 4


def adapter_layout(key):
    return jax.random.permutation(jax.random.fold_in(key, 5), ADAPTER_COUNT).astype(jnp.int32)


def draw_adapter_table_row(key, part):
    slots = adapter_layout(key)
    return slots


def draw_segment_adapter(key, part):
    slots = adapter_layout(key)
    holder = jnp.argsort(slots, stable=True).astype(jnp.int32)
    key = jax.random.fold_in(key, 12)
    owner_key, first_key, second_key = jax.random.split(key, 3)
    shard_keys = jax.random.split(owner_key, N_DP)
    owners = jax.vmap(lambda one: jax.random.permutation(one, N_DP)[:SEGS])(shard_keys).astype(jnp.int32)
    first = jax.random.randint(first_key, (N_DP, SEGS), 0, ADP_DEV)
    second = jax.random.randint(second_key, (N_DP, SEGS), 0, ADP_DEV)
    local = jnp.minimum(first, second).astype(jnp.int32)
    table_rows = owners * ADP_DEV + local
    return holder[table_rows.reshape(-1)].astype(jnp.int32)


def draw_segment_first_token(key, part):
    key = jax.random.fold_in(key, 13)
    shard_keys = jax.random.split(key, N_DP)

    def one_shard(one):
        cuts = jax.random.permutation(one, TOK_DP - 1)[:SEGS - 1].astype(jnp.int32) + 1
        cuts = jnp.sort(cuts)
        return jnp.concatenate([jnp.zeros((1,), jnp.int32), cuts])
    return jax.vmap(one_shard)(shard_keys).reshape(-1).astype(jnp.int32)


def block_scale(stream_key, shape, shards, smallest, high):
    gain, own = 1.0, jax.random.fold_in(stream_key, 6)
    for dim, blocks in shards:
        heights = jnp.exp(jax.random.uniform(jax.random.fold_in(own, dim), (blocks,), jnp.float32, smallest / len(shards), high / len(shards)))
        gain = gain * jnp.repeat(heights, shape[dim] // blocks).reshape([-1 if axis == dim else 1 for axis in range(len(shape))])
    return gain


def noise(stream_key, dims, width, limit, cuts=(), held_as=jnp.bfloat16):
    loudness = block_scale(stream_key, dims, cuts, -0.22, 0.18) if cuts else 1.0
    values = jax.random.normal(stream_key, dims, jnp.float32) * width * loudness
    return jnp.minimum(jnp.maximum(values, -limit), limit).astype(held_as)


def setup_inputs(seed: int = 0, part: int = 0) -> dict:
    arg_keys = jax.random.split(jax.random.key(seed), 9)
    part_splits = jax.random.split(jax.random.fold_in(arg_keys[8], part), 9)
    output_gradient = noise(part_splits[0], (TOKENS, MODEL_WIDTH), 0.5, 4.0, ((0, 4), (1, 4)))
    attention_output = noise(part_splits[1], (TOKENS, INPUT_FEATURES), 1.0, 6.0, ((0, 4), (1, 4)))
    frozen_weight = noise(arg_keys[2], (INPUT_FEATURES, MODEL_WIDTH), MODEL_WIDTH ** -0.5, 0.0625, ((0, 4), (1, 4)))
    adapter_down_table = noise(part_splits[3], (ADAPTER_COUNT, INPUT_FEATURES, ADAPTER_RANK), ADAPTER_RANK ** -0.5, 1.5, ((0, 4), (1, 4)))
    adapter_up_table = noise(part_splits[4], (ADAPTER_COUNT, ADAPTER_RANK, MODEL_WIDTH), MODEL_WIDTH ** -0.5, 0.0625, ((0, 4), (2, 4)))
    segment_adapter = draw_segment_adapter(jax.random.fold_in(jax.random.fold_in(arg_keys[8], part), 71), part)
    segment_first_token = draw_segment_first_token(jax.random.fold_in(jax.random.fold_in(arg_keys[8], part), 71), part)
    adapter_table_row = draw_adapter_table_row(jax.random.fold_in(jax.random.fold_in(arg_keys[8], part), 71), part)
    return dict(output_gradient=output_gradient, attention_output=attention_output, frozen_weight=frozen_weight, adapter_down_table=adapter_down_table, adapter_up_table=adapter_up_table, segment_adapter=segment_adapter, segment_first_token=segment_first_token, adapter_table_row=adapter_table_row)


adapter_scale = 2.0


def reference(output_gradient, attention_output, frozen_weight, adapter_down_table, adapter_up_table, segment_adapter, segment_first_token, adapter_table_row):
    rows = adapter_table_row[segment_adapter].astype(jnp.int32).reshape(N_DP, SEGS)
    starts = segment_first_token.reshape(N_DP, SEGS)
    grads = output_gradient.reshape(N_DP, TOK_DP, MODEL_WIDTH)
    inputs = attention_output.reshape(N_DP, TOK_DP, INPUT_FEATURES)

    def one_shard(operands):
        gradient_kept, input_kept, rows_kept, start_k = operands
        places = jnp.arange(TOK_DP, dtype=jnp.int32)
        seg_of = jnp.sum((places[:, None] >= start_k[None, :]).astype(jnp.int32), axis=1) - 1
        member = seg_of[:, None] == jnp.arange(SEGS, dtype=jnp.int32)[None, :]
        down_factor = adapter_down_table[rows_kept].astype(jnp.float32)
        up_factor = adapter_up_table[rows_kept].astype(jnp.float32)
        up_proj = jnp.einsum("td,srd->tsr", gradient_kept.astype(jnp.float32), up_factor)
        down_proj = jnp.einsum("th,shr->tsr", input_kept.astype(jnp.float32), down_factor)
        up_factor_block = jnp.where(member[:, :, None], up_proj, 0.0).astype(jnp.bfloat16)
        down_factor_block = jnp.where(member[:, :, None], down_proj, 0.0).astype(jnp.bfloat16)
        adapter_extra = adapter_scale * jnp.einsum("uzj,zaj->ua", up_factor_block.astype(jnp.float32), down_factor)
        segment_down = (adapter_scale * jnp.einsum("vf,veo->efo", input_kept.astype(jnp.float32), up_factor_block.astype(jnp.float32))).astype(jnp.bfloat16)
        segment_up = (adapter_scale * jnp.einsum("pho,py->hoy", down_factor_block.astype(jnp.float32), gradient_kept.astype(jnp.float32))).astype(jnp.bfloat16)
        return adapter_extra, segment_down, segment_up

    adapter_extra, segment_down, segment_up = lax.map(one_shard, (grads, inputs, rows, starts))
    frozen_output = jnp.dot(output_gradient, frozen_weight.T, preferred_element_type=jnp.float32)
    input_gradient = (frozen_output + adapter_extra.reshape(TOKENS, INPUT_FEATURES)).astype(jnp.bfloat16)
    flat_rows = rows.reshape(-1)
    grad_a = jnp.zeros((ADAPTER_COUNT, INPUT_FEATURES, ADAPTER_RANK), jnp.float32).at[flat_rows].add(segment_down.reshape(-1, INPUT_FEATURES, ADAPTER_RANK).astype(jnp.float32)).astype(jnp.bfloat16)
    grad_b = jnp.zeros((ADAPTER_COUNT, ADAPTER_RANK, MODEL_WIDTH), jnp.float32).at[flat_rows].add(segment_up.reshape(-1, ADAPTER_RANK, MODEL_WIDTH).astype(jnp.float32)).astype(jnp.bfloat16)
    return input_gradient, grad_a, grad_b
```

```python
import jax
import jax.numpy as jnp
from jax import lax
from jax.sharding import PartitionSpec as P

adapter_scale = 2.0


def local(
    output_gradient,
    attention_output,
    frozen_weight,
    adapter_down_table,
    adapter_up_table,
    segment_adapter,
    segment_first_token,
    adapter_table_row,
):
    n_dp = lax.axis_size("dp")
    segs = segment_adapter.shape[0]
    tok_rows = output_gradient.shape[0]
    adapters_per_device, features_local, rank_width = adapter_down_table.shape
    width_local = adapter_up_table.shape[2]
    brain_float_half = jnp.bfloat16
    hits = (
        segment_adapter[:, None] == jnp.arange(adapter_table_row.shape[0], dtype=jnp.int32)[None, :]
    )
    table_rows = jnp.sum(jnp.where(hits, adapter_table_row[None, :], 0), axis=1)
    owners = table_rows // adapters_per_device
    local_rows = table_rows % adapters_per_device
    to_owner = owners[:, None] == jnp.arange(n_dp, dtype=jnp.int32)[None, :]
    asked = jnp.sum(jnp.where(to_owner, (local_rows + 1)[:, None], 0), axis=0)
    wanted = lax.all_to_all(asked, "dp", split_axis=0, concat_axis=0, tiled=True)
    segment_selector = (
        wanted[:, None] - 1 == jnp.arange(adapters_per_device, dtype=jnp.int32)[None, :]
    ).astype(brain_float_half)
    send_a = jnp.dot(
        segment_selector,
        adapter_down_table.reshape(adapters_per_device, features_local * rank_width),
        preferred_element_type=jnp.float32,
    ).astype(brain_float_half)
    send_b = jnp.dot(
        segment_selector,
        adapter_up_table.reshape(adapters_per_device, rank_width * width_local),
        preferred_element_type=jnp.float32,
    ).astype(brain_float_half)
    got_a, got_b = (
        lax.all_to_all(send_a, "dp", split_axis=0, concat_axis=0, tiled=True),
        lax.all_to_all(send_b, "dp", split_axis=0, concat_axis=0, tiled=True),
    )
    chooser = to_owner.astype(brain_float_half)
    seg_factor_a = (
        jnp.dot(chooser, got_a, preferred_element_type=jnp.float32)
        .astype(brain_float_half)
        .reshape(segs, features_local, rank_width)
    )
    stacked_b = (
        jnp.dot(chooser, got_b, preferred_element_type=jnp.float32)
        .astype(brain_float_half)
        .reshape(segs * rank_width, width_local)
    )
    stacked_a = jnp.transpose(seg_factor_a, (1, 0, 2)).reshape(features_local, segs * rank_width)
    places = jnp.arange(tok_rows, dtype=jnp.int32)
    seg_of = (
        jnp.sum((places[:, None] >= segment_first_token[None, :]).astype(jnp.int32), axis=1) - 1
    )
    member = seg_of[:, None] == jnp.arange(segs, dtype=jnp.int32)[None, :]
    member_cols = jnp.repeat(member, rank_width, axis=1)
    up_part = lax.dot_general(
        output_gradient, stacked_b, (((1,), (1,)), ((), ())), preferred_element_type=jnp.float32
    )
    down_part = jnp.dot(attention_output, stacked_a, preferred_element_type=jnp.float32)
    up_proj, down_proj = lax.psum((up_part, down_part), ("fsdp", "adapter"))
    up_factor_block = jnp.where(member_cols, up_proj, 0.0).astype(brain_float_half)
    down_factor_block = jnp.where(member_cols, down_proj, 0.0).astype(brain_float_half)
    n_feat = lax.axis_size(("fsdp", "adapter"))
    part_rows = tok_rows // n_feat
    row_part = lax.all_to_all(
        output_gradient, ("fsdp", "adapter"), split_axis=0, concat_axis=1, tiled=True
    )
    row_part = lax.all_to_all(row_part, "dp", split_axis=1, concat_axis=0, tiled=True)
    all_rows = lax.all_gather(row_part, ("fsdp", "adapter"), axis=0, tiled=True)
    partial_output = lax.dot_general(
        all_rows, frozen_weight, (((1,), (1,)), ((), ())), preferred_element_type=jnp.float32
    ).astype(brain_float_half)
    partial_output = jnp.transpose(
        partial_output.reshape(n_feat, n_dp, part_rows, features_local), (1, 0, 2, 3)
    ).reshape(n_dp * tok_rows, features_local)
    partial_output = lax.all_to_all(
        partial_output, "dp", split_axis=0, concat_axis=0, tiled=True
    ).reshape(n_dp, tok_rows, features_local)
    frozen_output = jnp.sum(partial_output.astype(jnp.float32), axis=0)
    adapter_extra = lax.dot_general(
        up_factor_block, stacked_a, (((1,), (1,)), ((), ())), preferred_element_type=jnp.float32
    )
    input_gradient = (frozen_output + adapter_scale * adapter_extra).astype(brain_float_half)
    seg_grad_a = (
        adapter_scale
        * lax.dot_general(
            attention_output,
            up_factor_block,
            (((0,), (0,)), ((), ())),
            preferred_element_type=jnp.float32,
        )
    ).astype(brain_float_half)
    seg_grad_a = jnp.transpose(
        seg_grad_a.reshape(features_local, segs, rank_width), (1, 0, 2)
    ).reshape(segs, features_local * rank_width)
    seg_grad_b = (
        adapter_scale
        * lax.dot_general(
            down_factor_block,
            output_gradient,
            (((0,), (0,)), ((), ())),
            preferred_element_type=jnp.float32,
        )
    ).astype(brain_float_half)
    seg_grad_b = seg_grad_b.reshape(segs, rank_width * width_local)
    placer = jnp.transpose(chooser)
    out_a = jnp.dot(placer, seg_grad_a, preferred_element_type=jnp.float32).astype(brain_float_half)
    out_b = jnp.dot(placer, seg_grad_b, preferred_element_type=jnp.float32).astype(brain_float_half)
    back_a, back_b = (
        lax.all_to_all(out_a, "dp", split_axis=0, concat_axis=0, tiled=True),
        lax.all_to_all(out_b, "dp", split_axis=0, concat_axis=0, tiled=True),
    )
    gatherer = jnp.transpose(segment_selector)
    grad_a = (
        jnp.dot(gatherer, back_a, preferred_element_type=jnp.float32)
        .astype(brain_float_half)
        .reshape(adapters_per_device, features_local, rank_width)
    )
    grad_b = (
        jnp.dot(gatherer, back_b, preferred_element_type=jnp.float32)
        .astype(brain_float_half)
        .reshape(adapters_per_device, rank_width, width_local)
    )
    return (input_gradient, grad_a, grad_b)


def solution(mesh):
    in_specs = (
        P(("groups", "dp"), ("fsdp", "adapter")),
        P(("groups", "dp"), ("fsdp", "adapter")),
        P(("fsdp", "adapter"), "dp"),
        P(("groups", "dp"), ("fsdp", "adapter"), None),
        P(("groups", "dp"), None, ("fsdp", "adapter")),
        P(("groups", "dp")),
        P(("groups", "dp")),
        P("groups"),
    )
    out_specs = (
        P(("groups", "dp"), ("fsdp", "adapter")),
        P(("groups", "dp"), ("fsdp", "adapter"), None),
        P(("groups", "dp"), None, ("fsdp", "adapter")),
    )
    return jax.shard_map(local, mesh=mesh, in_specs=in_specs, out_specs=out_specs, check_vma=False)
```

```python
import functools

import jax
import jax.numpy as jnp
from jax import lax
from jax.experimental import pallas as pl
from jax.experimental.pallas import tpu as pltpu
from jax.sharding import PartitionSpec as P

adapter_scale = 2.0
float_half = jnp.bfloat16
both_minor = (((1,), (1,)), ((), ()))
both_major = (((0,), (0,)), ((), ()))


def flip(index, step):
    out, bit = index, 1
    while bit <= step:
        if step & bit:
            out = out + bit - 2 * bit * ((index // bit) % 2)
        bit *= 2
    return out


def copy_to(src, dst, send_sem, recv_sem, device):
    return pltpu.make_async_remote_copy(
        src_ref=src,
        dst_ref=dst,
        send_sem=send_sem,
        recv_sem=recv_sem,
        device_id=device,
        device_id_type=pl.DeviceIdType.MESH,
    )


def kernel(
    n_dp,
    n_fsdp,
    n_core,
    rank,
    grad_ref,
    act_ref,
    weight_hbm,
    down_hbm,
    up_hbm,
    asked_ref,
    key_ref,
    mask_ref,
    out_ref,
    back_ref,
    sel_ref,
    weight,
    down,
    up,
    asked_in,
    factor_out,
    factor_in,
    proj_out,
    proj_in,
    back_out,
    back_in,
    rows_in,
    grad_all,
    part_out,
    part_in,
    total,
    load_sem,
    asked_s,
    asked_r,
    factor_s,
    factor_r,
    proj_s,
    proj_r,
    back_s,
    back_r,
    rows_s,
    rows_r,
    grad_s,
    grad_r,
    cross_s,
    cross_r,
    core_s,
    core_r,
    part_s,
    part_r,
):
    dp, fsdp, core = lax.axis_index("dp"), lax.axis_index("fsdp"), lax.axis_index("adapter")
    feat = fsdp * n_core + core
    n_feat = n_fsdp * n_core
    tok, width = grad_ref.shape
    feats = act_ref.shape[1]
    rows = tok // n_feat
    width_dp = grad_all.shape[2]
    per_feat = n_dp // n_feat

    def feat_device(index):
        return {"fsdp": index // n_core, "adapter": index % n_core}

    def rank_rows(index):
        return pl.ds(pl.multiple_of(index * rank, rank), rank)

    def token_rows(index):
        return pl.ds(pl.multiple_of(index * rows, rows), rows)

    loads = [
        pltpu.make_async_copy(src, dst, load_sem.at[i])
        for i, (src, dst) in enumerate(((down_hbm, down), (up_hbm, up), (weight_hbm, weight)))
    ]
    for load in loads:
        load.start()

    barrier = pltpu.get_barrier_semaphore()
    for step in range(1, n_dp):
        pl.semaphore_signal(
            barrier,
            inc=1,
            device_id={"dp": flip(dp, step)},
            device_id_type=pl.DeviceIdType.MESH,
        )
    for step in range(1, n_feat):
        pl.semaphore_signal(
            barrier,
            inc=1,
            device_id=feat_device(flip(feat, step)),
            device_id_type=pl.DeviceIdType.MESH,
        )
    pl.semaphore_wait(barrier, n_dp + n_feat - 2)

    def dp_exchange(step, src, dst, send, recv):
        peer = flip(dp, step)
        return copy_to(
            src.at[rank_rows(peer)],
            dst.at[rank_rows(dp)],
            send.at[peer],
            recv.at[dp],
            {"dp": peer},
        )

    def dp_arrival(step, src, dst, send, recv):
        peer = flip(dp, step)
        return copy_to(
            src.at[rank_rows(peer)],
            dst.at[rank_rows(peer)],
            send.at[peer],
            recv.at[peer],
            {"dp": peer},
        )

    asked_args = (asked_ref, asked_in, asked_s, asked_r)
    factor_args = (factor_out, factor_in, factor_s, factor_r)
    back_args = (back_out, back_in, back_s, back_r)

    for step in range(1, n_dp):
        dp_exchange(step, *asked_args).start()
    asked_in[rank_rows(dp), :] = asked_ref[rank_rows(dp), :]

    def rows_copy(step):
        peer = flip(feat, step)
        return copy_to(
            grad_ref.at[token_rows(peer)],
            rows_in.at[feat],
            rows_s.at[peer],
            rows_r.at[feat],
            feat_device(peer),
        )

    def rows_arrival(step):
        peer = flip(feat, step)
        return copy_to(
            grad_ref.at[token_rows(peer)],
            rows_in.at[peer],
            rows_s.at[peer],
            rows_r.at[peer],
            feat_device(peer),
        )

    for step in range(1, n_feat):
        rows_copy(step).start()

    def grad_copy(step, part):
        source = flip(feat, step)
        target = source * per_feat + part
        columns = pl.ds(part * width_dp, width_dp)
        if step == 0:
            block = grad_ref.at[token_rows(feat), columns]
        else:
            block = rows_in.at[source, :, columns]
        copy = copy_to(
            block,
            grad_all.at[dp, token_rows(feat)],
            grad_s.at[target],
            grad_r.at[dp],
            {"dp": target},
        )
        return target, block, copy

    def forward(step):
        for part in range(per_feat):
            target, block, copy = grad_copy(step, part)

            @pl.when(target != dp)
            def _():
                copy.start()

            @pl.when(target == dp)
            def _():
                grad_all[dp, token_rows(feat), :] = block[...]

    forward(0)

    loads[0].wait()
    loads[1].wait()
    for step in range(1, n_dp):
        dp_arrival(step, *asked_args).wait_recv()
    chosen = jnp.where(asked_in[...] - 1 == key_ref[...], 1.0, 0.0).astype(float_half)
    sel_ref[...] = chosen
    factor_out[:, :feats] = jnp.dot(
        chosen, down[...], preferred_element_type=jnp.float32
    ).astype(float_half)
    factor_out[:, feats:] = jnp.dot(
        chosen, up[...], preferred_element_type=jnp.float32
    ).astype(float_half)
    for step in range(1, n_dp):
        dp_exchange(step, *factor_args).start()
    factor_in[rank_rows(dp), :] = factor_out[rank_rows(dp), :]

    for step in range(1, n_feat):
        rows_arrival(step).wait_recv()
        forward(step)

    def proj_copy(step):
        peer = flip(feat, step)
        return copy_to(
            proj_out, proj_in.at[feat], proj_s.at[peer], proj_r.at[feat], feat_device(peer)
        )

    def proj_arrival(step):
        peer = flip(feat, step)
        return copy_to(
            proj_out, proj_in.at[peer], proj_s.at[peer], proj_r.at[peer], feat_device(peer)
        )

    def in_owner(owner):
        return mask_ref[owner : owner + 1, :] > 0.0

    def project():
        for step in range(1, n_dp):
            dp_arrival(step, *factor_args).wait_recv()
        for half, (factor, value) in enumerate(
            ((factor_in[:, feats:], grad_ref[...]), (factor_in[:, :feats], act_ref[...]))
        ):
            product = lax.dot_general(
                factor, value, both_minor, preferred_element_type=jnp.float32
            )
            folded = jnp.zeros((rank, tok), jnp.float32)
            for owner in range(n_dp):
                folded += jnp.where(
                    in_owner(owner), product[owner * rank : (owner + 1) * rank], 0.0
                )
            proj_out[half * rank : (half + 1) * rank, :] = folded
        for step in range(1, n_feat):
            proj_copy(step).start()
        proj_in[feat] = proj_out[...]

    def adapter_gradients():
        for step in range(1, n_feat):
            proj_arrival(step).wait_recv()
        summed = proj_in[0]
        for index in range(1, n_feat):
            summed += proj_in[index]

        def spread(values):
            return jnp.concatenate(
                [jnp.where(in_owner(owner), values, 0.0) for owner in range(n_dp)], axis=0
            ).astype(float_half)

        up_block, down_block = spread(summed[:rank]), spread(summed[rank:])
        back_out[:, :feats] = (
            adapter_scale
            * jnp.dot(up_block, act_ref[...], preferred_element_type=jnp.float32)
        ).astype(float_half)
        back_out[:, feats:] = (
            adapter_scale
            * jnp.dot(down_block, grad_ref[...], preferred_element_type=jnp.float32)
        ).astype(float_half)
        for step in range(1, n_dp):
            dp_exchange(step, *back_args).start()
        back_in[rank_rows(dp), :] = back_out[rank_rows(dp), :]
        total[...] += adapter_scale * lax.dot_general(
            up_block, factor_in[:, :feats], both_major, preferred_element_type=jnp.float32
        )

    def grad_arrival(step):
        peer = flip(dp, step)
        block = grad_all.at[peer, token_rows(feat)]
        return copy_to(block, block, grad_s.at[peer], grad_r.at[peer], {"dp": peer})

    def cross_copy(index, step):
        peer = flip(fsdp, step)
        block = grad_all.at[index, token_rows(feat)]
        return copy_to(
            block, block, cross_s.at[index, peer], cross_r.at[index, fsdp], {"fsdp": peer}
        )

    def cross_arrival(index, step):
        peer = flip(fsdp, step)
        block = grad_all.at[index, token_rows(peer * n_core + core)]
        return copy_to(
            block, block, cross_s.at[index, peer], cross_r.at[index, peer], {"fsdp": peer}
        )

    def core_copy(index, step, side):
        chip, peer = flip(fsdp, step), flip(core, side)
        block = grad_all.at[index, token_rows(chip * n_core + core)]
        return copy_to(
            block,
            block,
            core_s.at[index, chip, peer],
            core_r.at[index, chip, core],
            {"adapter": peer},
        )

    def core_arrival(index, step, side):
        chip, peer = flip(fsdp, step), flip(core, side)
        block = grad_all.at[index, token_rows(chip * n_core + peer)]
        return copy_to(
            block,
            block,
            core_s.at[index, chip, peer],
            core_r.at[index, chip, peer],
            {"adapter": peer},
        )

    def part_copy(step):
        peer = flip(dp, step)
        return copy_to(
            part_out.at[peer], part_in.at[dp], part_s.at[peer], part_r.at[dp], {"dp": peer}
        )

    def part_arrival(step):
        peer = flip(dp, step)
        return copy_to(
            part_out.at[peer], part_in.at[peer], part_s.at[peer], part_r.at[peer], {"dp": peer}
        )

    tile = 256 if feats % 256 == 0 else feats

    def multiply(step):
        index = flip(dp, step)

        def one(i, carry):
            columns = pl.ds(pl.multiple_of(i * tile, tile), tile)
            product = lax.dot_general(
                grad_all[index], weight[columns, :], both_minor, preferred_element_type=jnp.float32
            )
            if step == 0:
                total[:, columns] = product
            else:
                part_out[index, :, columns] = product.astype(float_half)
            return carry

        lax.fori_loop(0, feats // tile, one, 0)
        if step:
            part_copy(step).start()

    for turn in range(n_dp + 2):
        if turn < n_dp:
            if turn:
                grad_arrival(turn).wait_recv()
            index = flip(dp, turn)
            for step in range(1, n_fsdp):
                cross_copy(index, step).start()
            for side in range(1, n_core):
                core_copy(index, 0, side).start()
        if turn == 0:
            project()
            loads[2].wait()
        if 1 <= turn <= n_dp:
            index = flip(dp, turn - 1)
            for step in range(1, n_fsdp):
                cross_arrival(index, step).wait_recv()
                for side in range(1, n_core):
                    core_copy(index, step, side).start()
        if turn >= 2:
            index = flip(dp, turn - 2)
            for step in range(n_fsdp):
                for side in range(1, n_core):
                    core_arrival(index, step, side).wait_recv()
            multiply(turn - 2)
        if turn == 2:
            adapter_gradients()

    for step in range(1, n_dp):
        part_arrival(step).wait_recv()
        total[...] += part_in[flip(dp, step)].astype(jnp.float32)
    out_ref[...] = total[...].astype(float_half)
    for step in range(1, n_dp):
        dp_arrival(step, *back_args).wait_recv()
    back_ref[...] = back_in[...]

    for step in range(1, n_dp):
        for args in (asked_args, factor_args, back_args):
            dp_exchange(step, *args).wait_send()
        part_copy(step).wait_send()
    for step in range(1, n_feat):
        rows_copy(step).wait_send()
        proj_copy(step).wait_send()
    for step in range(n_feat):
        for part in range(per_feat):
            target, _, copy = grad_copy(step, part)

            @pl.when(target != dp)
            def _():
                copy.wait_send()

    for turn in range(n_dp):
        index = flip(dp, turn)
        for step in range(1, n_fsdp):
            cross_copy(index, step).wait_send()
        for step in range(n_fsdp):
            for side in range(1, n_core):
                core_copy(index, step, side).wait_send()


def local(
    output_gradient,
    attention_output,
    frozen_weight,
    adapter_down_table,
    adapter_up_table,
    segment_adapter,
    segment_first_token,
    adapter_table_row,
):
    n_dp, n_fsdp, n_core = (lax.axis_size(name) for name in ("dp", "fsdp", "adapter"))
    n_feat = n_fsdp * n_core
    segs = segment_adapter.shape[0]
    tok, width = output_gradient.shape
    table, feats, rank = adapter_down_table.shape
    width_dp = frozen_weight.shape[1]
    hits = (
        segment_adapter[:, None] == jnp.arange(adapter_table_row.shape[0], dtype=jnp.int32)[None, :]
    )
    table_rows = jnp.sum(jnp.where(hits, adapter_table_row[None, :], 0), axis=1)
    owners = table_rows // table
    to_owner = owners[:, None] == jnp.arange(n_dp, dtype=jnp.int32)[None, :]
    asked = jnp.sum(jnp.where(to_owner, (table_rows % table + 1)[:, None], 0), axis=0)
    asked = jnp.broadcast_to(asked[:, None, None], (n_dp, rank, table * rank)).reshape(
        n_dp * rank, table * rank
    )
    row_of = lax.broadcasted_iota(jnp.int32, (n_dp * rank, table * rank), 0)
    col_of = lax.broadcasted_iota(jnp.int32, (n_dp * rank, table * rank), 1)
    key = jnp.where(row_of % rank == col_of % rank, col_of // rank, -5)
    places = jnp.arange(tok, dtype=jnp.int32)
    seg_of = (
        jnp.sum((places[:, None] >= segment_first_token[None, :]).astype(jnp.int32), axis=1) - 1
    )
    member = seg_of[None, :] == jnp.arange(segs, dtype=jnp.int32)[:, None]
    mask = jnp.sum(
        (to_owner[:, :, None] & member[:, None, :]).astype(jnp.float32), axis=0
    )
    down = jnp.transpose(adapter_down_table, (0, 2, 1)).reshape(table * rank, feats)
    up = adapter_up_table.reshape(table * rank, width)
    both = feats + width
    vmem = pl.BlockSpec(memory_space=pltpu.VMEM)
    hbm = pl.BlockSpec(memory_space=pl.ANY)
    dma = pltpu.SemaphoreType.DMA
    pair = [dma((n_dp,)), dma((n_dp,))]
    feat_pair = [dma((n_feat,)), dma((n_feat,))]
    input_gradient, back, chosen = pl.pallas_call(
        functools.partial(kernel, n_dp, n_fsdp, n_core, rank),
        out_shape=(
            jax.ShapeDtypeStruct((tok, feats), float_half),
            jax.ShapeDtypeStruct((n_dp * rank, both), float_half),
            jax.ShapeDtypeStruct((n_dp * rank, table * rank), float_half),
        ),
        in_specs=[vmem, vmem, hbm, hbm, hbm, vmem, vmem, vmem],
        out_specs=[vmem] * 3,
        scratch_shapes=[
            pltpu.VMEM((feats, width_dp), float_half),
            pltpu.VMEM((table * rank, feats), float_half),
            pltpu.VMEM((table * rank, width), float_half),
            pltpu.VMEM((n_dp * rank, table * rank), jnp.int32),
            pltpu.VMEM((n_dp * rank, both), float_half),
            pltpu.VMEM((n_dp * rank, both), float_half),
            pltpu.VMEM((2 * rank, tok), jnp.float32),
            pltpu.VMEM((n_feat, 2 * rank, tok), jnp.float32),
            pltpu.VMEM((n_dp * rank, both), float_half),
            pltpu.VMEM((n_dp * rank, both), float_half),
            pltpu.VMEM((n_feat, tok // n_feat, width), float_half),
            pltpu.VMEM((n_dp, tok, width_dp), float_half),
            pltpu.VMEM((n_dp, tok, feats), float_half),
            pltpu.VMEM((n_dp, tok, feats), float_half),
            pltpu.VMEM((tok, feats), jnp.float32),
            dma((3,)),
            *pair,
            *pair,
            *feat_pair,
            *pair,
            *feat_pair,
            *pair,
            dma((n_dp, n_fsdp)),
            dma((n_dp, n_fsdp)),
            dma((n_dp, n_fsdp, n_core)),
            dma((n_dp, n_fsdp, n_core)),
            *pair,
        ],
        compiler_params=pltpu.CompilerParams(
            collective_id=0, has_side_effects=True, vmem_limit_bytes=56 * 2**20
        ),
        cost_estimate=pl.CostEstimate(
            flops=2 * n_dp * tok * width_dp * feats,
            bytes_accessed=2 * (feats * width_dp + 2 * tok * (width + feats)),
            transcendentals=0,
        ),
    )(output_gradient, attention_output, frozen_weight, down, up, asked, key, mask)
    grad_a = lax.dot_general(
        chosen, back[:, :feats], both_major, preferred_element_type=jnp.float32
    ).astype(float_half)
    grad_b = lax.dot_general(
        chosen, back[:, feats:], both_major, preferred_element_type=jnp.float32
    ).astype(float_half)
    grad_a = jnp.transpose(grad_a.reshape(table, rank, feats), (0, 2, 1))
    return input_gradient, grad_a, grad_b.reshape(table, rank, width)


def solution(mesh):
    in_specs = (
        P(("groups", "dp"), ("fsdp", "adapter")),
        P(("groups", "dp"), ("fsdp", "adapter")),
        P(("fsdp", "adapter"), "dp"),
        P(("groups", "dp"), ("fsdp", "adapter"), None),
        P(("groups", "dp"), None, ("fsdp", "adapter")),
        P(("groups", "dp")),
        P(("groups", "dp")),
        P("groups"),
    )
    out_specs = (
        P(("groups", "dp"), ("fsdp", "adapter")),
        P(("groups", "dp"), ("fsdp", "adapter"), None),
        P(("groups", "dp"), None, ("fsdp", "adapter")),
    )
    return jax.shard_map(local, mesh=mesh, in_specs=in_specs, out_specs=out_specs, check_vma=False)
```

```python
import functools

import jax
import jax.numpy as jnp
from jax import lax
from jax.experimental import pallas as pl
from jax.experimental.pallas import tpu as pltpu
from jax.sharding import PartitionSpec as P

adapter_scale = 2.0
float_half = jnp.bfloat16
both_minor = (((1,), (1,)), ((), ()))
both_major = (((0,), (0,)), ((), ()))


def flip(index, step):
    out, bit = index, 1
    while bit <= step:
        if step & bit:
            out = out + bit - 2 * bit * ((index // bit) % 2)
        bit *= 2
    return out


def copy_to(src, dst, send_sem, recv_sem, device):
    return pltpu.make_async_remote_copy(
        src_ref=src,
        dst_ref=dst,
        send_sem=send_sem,
        recv_sem=recv_sem,
        device_id=device,
        device_id_type=pl.DeviceIdType.MESH,
    )


def kernel(
    n_dp,
    n_fsdp,
    n_core,
    rank,
    grad_ref,
    act_ref,
    weight_hbm,
    down_hbm,
    up_hbm,
    asked_ref,
    key_ref,
    mask_ref,
    out_ref,
    back_ref,
    sel_ref,
    weight,
    down,
    up,
    asked_in,
    factor_out,
    factor_in,
    proj_out,
    proj_in,
    back_out,
    back_in,
    rows_in,
    grad_all,
    part_out,
    part_in,
    product,
    total,
    load_sem,
    asked_s,
    asked_r,
    factor_s,
    factor_r,
    proj_s,
    proj_r,
    back_s,
    back_r,
    rows_s,
    rows_r,
    grad_s,
    grad_r,
    cross_s,
    cross_r,
    core_s,
    core_r,
    part_s,
    part_r,
):
    dp, fsdp, core = lax.axis_index("dp"), lax.axis_index("fsdp"), lax.axis_index("adapter")
    feat = fsdp * n_core + core
    n_feat = n_fsdp * n_core
    tok, width = grad_ref.shape
    feats = act_ref.shape[1]
    rows = tok // n_feat
    width_dp = grad_all.shape[2]
    per_feat = n_dp // n_feat

    def feat_device(index):
        return {"fsdp": index // n_core, "adapter": index % n_core}

    def rank_rows(index):
        return pl.ds(pl.multiple_of(index * rank, rank), rank)

    def token_rows(index):
        return pl.ds(pl.multiple_of(index * rows, rows), rows)

    loads = [
        pltpu.make_async_copy(src, dst, load_sem.at[i])
        for i, (src, dst) in enumerate(((down_hbm, down), (up_hbm, up), (weight_hbm, weight)))
    ]
    for load in loads:
        load.start()

    barrier = pltpu.get_barrier_semaphore()
    for step in range(1, n_dp):
        pl.semaphore_signal(
            barrier,
            inc=1,
            device_id={"dp": flip(dp, step)},
            device_id_type=pl.DeviceIdType.MESH,
        )
    for step in range(1, n_feat):
        pl.semaphore_signal(
            barrier,
            inc=1,
            device_id=feat_device(flip(feat, step)),
            device_id_type=pl.DeviceIdType.MESH,
        )
    pl.semaphore_wait(barrier, n_dp + n_feat - 2)

    def dp_exchange(step, src, dst, send, recv):
        peer = flip(dp, step)
        return copy_to(
            src.at[rank_rows(peer)],
            dst.at[rank_rows(dp)],
            send.at[peer],
            recv.at[dp],
            {"dp": peer},
        )

    def dp_arrival(step, src, dst, send, recv):
        peer = flip(dp, step)
        return copy_to(
            src.at[rank_rows(peer)],
            dst.at[rank_rows(peer)],
            send.at[peer],
            recv.at[peer],
            {"dp": peer},
        )

    asked_args = (asked_ref, asked_in, asked_s, asked_r)
    factor_args = (factor_out, factor_in, factor_s, factor_r)
    back_args = (back_out, back_in, back_s, back_r)

    for step in range(1, n_dp):
        dp_exchange(step, *asked_args).start()
    asked_in[rank_rows(dp), :] = asked_ref[rank_rows(dp), :]

    def rows_copy(step):
        peer = flip(feat, step)
        return copy_to(
            grad_ref.at[token_rows(peer)],
            rows_in.at[feat],
            rows_s.at[peer],
            rows_r.at[feat],
            feat_device(peer),
        )

    def rows_arrival(step):
        peer = flip(feat, step)
        return copy_to(
            grad_ref.at[token_rows(peer)],
            rows_in.at[peer],
            rows_s.at[peer],
            rows_r.at[peer],
            feat_device(peer),
        )

    for step in range(1, n_feat):
        rows_copy(step).start()

    def grad_copy(step, part):
        source = flip(feat, step)
        target = source * per_feat + part
        columns = pl.ds(part * width_dp, width_dp)
        if step == 0:
            block = grad_ref.at[token_rows(feat), columns]
        else:
            block = rows_in.at[source, :, columns]
        copy = copy_to(
            block,
            grad_all.at[dp, token_rows(feat)],
            grad_s.at[target],
            grad_r.at[dp],
            {"dp": target},
        )
        return target, block, copy

    def forward(step):
        for part in range(per_feat):
            target, block, copy = grad_copy(step, part)

            @pl.when(target != dp)
            def _():
                copy.start()

            @pl.when(target == dp)
            def _():
                grad_all[dp, token_rows(feat), :] = block[...]

    forward(0)

    loads[0].wait()
    loads[1].wait()
    for step in range(1, n_dp):
        dp_arrival(step, *asked_args).wait_recv()
    chosen = jnp.where(asked_in[...] - 1 == key_ref[...], 1.0, 0.0).astype(float_half)
    sel_ref[...] = chosen
    factor_out[:, :feats] = jnp.dot(
        chosen, down[...], preferred_element_type=jnp.float32
    ).astype(float_half)
    factor_out[:, feats:] = jnp.dot(
        chosen, up[...], preferred_element_type=jnp.float32
    ).astype(float_half)
    for step in range(1, n_dp):
        dp_exchange(step, *factor_args).start()
    factor_in[rank_rows(dp), :] = factor_out[rank_rows(dp), :]

    for step in range(1, n_feat):
        rows_arrival(step).wait_recv()
        forward(step)

    def proj_copy(step):
        peer = flip(feat, step)
        return copy_to(
            proj_out, proj_in.at[feat], proj_s.at[peer], proj_r.at[feat], feat_device(peer)
        )

    def proj_arrival(step):
        peer = flip(feat, step)
        return copy_to(
            proj_out, proj_in.at[peer], proj_s.at[peer], proj_r.at[peer], feat_device(peer)
        )

    def in_owner(owner):
        return mask_ref[owner : owner + 1, :] > 0.0

    def project():
        for step in range(1, n_dp):
            dp_arrival(step, *factor_args).wait_recv()
        for half, (factor, value) in enumerate(
            ((factor_in[:, feats:], grad_ref[...]), (factor_in[:, :feats], act_ref[...]))
        ):
            product = lax.dot_general(
                factor, value, both_minor, preferred_element_type=jnp.float32
            )
            folded = jnp.zeros((rank, tok), jnp.float32)
            for owner in range(n_dp):
                folded += jnp.where(
                    in_owner(owner), product[owner * rank : (owner + 1) * rank], 0.0
                )
            proj_out[half * rank : (half + 1) * rank, :] = folded
        for step in range(1, n_feat):
            proj_copy(step).start()
        proj_in[feat] = proj_out[...]

    def adapter_gradients():
        for step in range(1, n_feat):
            proj_arrival(step).wait_recv()
        summed = proj_in[0]
        for index in range(1, n_feat):
            summed += proj_in[index]

        def spread(values):
            return jnp.concatenate(
                [jnp.where(in_owner(owner), values, 0.0) for owner in range(n_dp)], axis=0
            ).astype(float_half)

        up_block, down_block = spread(summed[:rank]), spread(summed[rank:])
        back_out[:, :feats] = (
            adapter_scale
            * jnp.dot(up_block, act_ref[...], preferred_element_type=jnp.float32)
        ).astype(float_half)
        back_out[:, feats:] = (
            adapter_scale
            * jnp.dot(down_block, grad_ref[...], preferred_element_type=jnp.float32)
        ).astype(float_half)
        for step in range(1, n_dp):
            dp_exchange(step, *back_args).start()
        back_in[rank_rows(dp), :] = back_out[rank_rows(dp), :]
        total[...] += adapter_scale * lax.dot_general(
            up_block, factor_in[:, :feats], both_major, preferred_element_type=jnp.float32
        )

    def grad_arrival(peer):
        block = grad_all.at[peer, token_rows(feat)]
        return copy_to(block, block, grad_s.at[peer], grad_r.at[peer], {"dp": peer})

    def cross_copy(index, step):
        peer = flip(fsdp, step)
        block = grad_all.at[index, token_rows(feat)]
        return copy_to(
            block, block, cross_s.at[index, peer], cross_r.at[index, fsdp], {"fsdp": peer}
        )

    def cross_arrival(index, step):
        peer = flip(fsdp, step)
        block = grad_all.at[index, token_rows(peer * n_core + core)]
        return copy_to(
            block, block, cross_s.at[index, peer], cross_r.at[index, peer], {"fsdp": peer}
        )

    def core_copy(index, step, side):
        chip, peer = flip(fsdp, step), flip(core, side)
        block = grad_all.at[index, token_rows(chip * n_core + core)]
        return copy_to(
            block,
            block,
            core_s.at[index, chip, peer],
            core_r.at[index, chip, core],
            {"adapter": peer},
        )

    def core_arrival(index, step, side):
        chip, peer = flip(fsdp, step), flip(core, side)
        block = grad_all.at[index, token_rows(chip * n_core + peer)]
        return copy_to(
            block,
            block,
            core_s.at[index, chip, peer],
            core_r.at[index, chip, peer],
            {"adapter": peer},
        )

    def order(turn):
        if turn == 0:
            return dp
        upper = dp // (n_dp // 2)
        falling, rising = n_dp - turn, turn - 1
        falling = falling - (dp - falling + n_dp) // n_dp
        rising = rising + (rising - dp + n_dp) // n_dp
        return (1 - upper) * falling + upper * rising

    def part_copy(turn):
        index = order(turn)
        above = (index - dp - 1 + n_dp) // n_dp
        following = dp + 2 * above - 1
        ends = (1 - above) * (1 - (following - index + n_dp - 1) // n_dp)
        slot = index + ends * (n_dp - index)
        return copy_to(
            part_out.at[index],
            part_in.at[slot],
            part_s.at[index],
            part_r.at[slot],
            {"dp": following},
        )

    def part_arrival(slot):
        return copy_to(
            part_out.at[0], part_in.at[slot], part_s.at[0], part_r.at[slot], {"dp": flip(dp, 1)}
        )

    tile = 256 if feats % 256 == 0 else feats

    def multiply(index, store):
        def one(i, carry):
            columns = pl.ds(pl.multiple_of(i * tile, tile), tile)
            store(
                columns,
                lax.dot_general(
                    grad_all[index],
                    weight[columns, :],
                    both_minor,
                    preferred_element_type=jnp.float32,
                ),
            )
            return carry

        lax.fori_loop(0, feats // tile, one, 0)

    outermost = dp * (n_dp - 1 - dp) == 0

    def begin_chain(turn):
        index = order(turn)

        def store(columns, value):
            part_out[index, :, columns] = value.astype(float_half)

        @pl.when(outermost)
        def _():
            multiply(index, store)
            part_copy(turn).start()

    def continue_chain(turn):
        index = order(turn)

        def store(columns, value):
            product[:, columns] = value

        @pl.when(jnp.logical_not(outermost))
        def _():
            multiply(index, store)
            part_arrival(index).wait_recv()
            part_out[index] = (product[...] + part_in[index].astype(jnp.float32)).astype(
                float_half
            )
            part_copy(turn).start()

    def own_product():
        def store(columns, value):
            total[:, columns] = value

        multiply(dp, store)

    for turn in range(n_dp + 2):
        if turn < n_dp:
            index = order(turn)
            if turn:
                grad_arrival(index).wait_recv()
            for step in range(1, n_fsdp):
                cross_copy(index, step).start()
            for side in range(1, n_core):
                core_copy(index, 0, side).start()
        if turn == 0:
            project()
            loads[2].wait()
        if 1 <= turn <= n_dp:
            index = order(turn - 1)
            for step in range(1, n_fsdp):
                cross_arrival(index, step).wait_recv()
                for side in range(1, n_core):
                    core_copy(index, step, side).start()
        if turn >= 2:
            index = order(turn - 2)
            for step in range(n_fsdp):
                for side in range(1, n_core):
                    core_arrival(index, step, side).wait_recv()
            if turn == 2:
                own_product()
                adapter_gradients()
            else:
                begin_chain(turn - 2)

    for turn in range(1, n_dp):
        continue_chain(turn)

    for slot, there in ((dp, dp > 0), (n_dp, dp < n_dp - 1)):

        @pl.when(there)
        def _():
            part_arrival(slot).wait_recv()
            total[...] += part_in[slot].astype(jnp.float32)

    out_ref[...] = total[...].astype(float_half)
    for step in range(1, n_dp):
        dp_arrival(step, *back_args).wait_recv()
    back_ref[...] = back_in[...]

    for step in range(1, n_dp):
        for args in (asked_args, factor_args, back_args):
            dp_exchange(step, *args).wait_send()
        part_copy(step).wait_send()
    for step in range(1, n_feat):
        rows_copy(step).wait_send()
        proj_copy(step).wait_send()
    for step in range(n_feat):
        for part in range(per_feat):
            target, _, copy = grad_copy(step, part)

            @pl.when(target != dp)
            def _():
                copy.wait_send()

    for turn in range(n_dp):
        index = flip(dp, turn)
        for step in range(1, n_fsdp):
            cross_copy(index, step).wait_send()
        for step in range(n_fsdp):
            for side in range(1, n_core):
                core_copy(index, step, side).wait_send()


def local(
    output_gradient,
    attention_output,
    frozen_weight,
    adapter_down_table,
    adapter_up_table,
    segment_adapter,
    segment_first_token,
    adapter_table_row,
):
    n_dp, n_fsdp, n_core = (lax.axis_size(name) for name in ("dp", "fsdp", "adapter"))
    n_feat = n_fsdp * n_core
    segs = segment_adapter.shape[0]
    tok, width = output_gradient.shape
    table, feats, rank = adapter_down_table.shape
    width_dp = frozen_weight.shape[1]
    hits = (
        segment_adapter[:, None] == jnp.arange(adapter_table_row.shape[0], dtype=jnp.int32)[None, :]
    )
    table_rows = jnp.sum(jnp.where(hits, adapter_table_row[None, :], 0), axis=1)
    owners = table_rows // table
    to_owner = owners[:, None] == jnp.arange(n_dp, dtype=jnp.int32)[None, :]
    asked = jnp.sum(jnp.where(to_owner, (table_rows % table + 1)[:, None], 0), axis=0)
    asked = jnp.broadcast_to(asked[:, None, None], (n_dp, rank, table * rank)).reshape(
        n_dp * rank, table * rank
    )
    row_of = lax.broadcasted_iota(jnp.int32, (n_dp * rank, table * rank), 0)
    col_of = lax.broadcasted_iota(jnp.int32, (n_dp * rank, table * rank), 1)
    key = jnp.where(row_of % rank == col_of % rank, col_of // rank, -5)
    places = jnp.arange(tok, dtype=jnp.int32)
    seg_of = (
        jnp.sum((places[:, None] >= segment_first_token[None, :]).astype(jnp.int32), axis=1) - 1
    )
    member = seg_of[None, :] == jnp.arange(segs, dtype=jnp.int32)[:, None]
    mask = jnp.sum(
        (to_owner[:, :, None] & member[:, None, :]).astype(jnp.float32), axis=0
    )
    down = jnp.transpose(adapter_down_table, (0, 2, 1)).reshape(table * rank, feats)
    up = adapter_up_table.reshape(table * rank, width)
    both = feats + width
    vmem = pl.BlockSpec(memory_space=pltpu.VMEM)
    hbm = pl.BlockSpec(memory_space=pl.ANY)
    dma = pltpu.SemaphoreType.DMA
    pair = [dma((n_dp,)), dma((n_dp,))]
    feat_pair = [dma((n_feat,)), dma((n_feat,))]
    input_gradient, back, chosen = pl.pallas_call(
        functools.partial(kernel, n_dp, n_fsdp, n_core, rank),
        out_shape=(
            jax.ShapeDtypeStruct((tok, feats), float_half),
            jax.ShapeDtypeStruct((n_dp * rank, both), float_half),
            jax.ShapeDtypeStruct((n_dp * rank, table * rank), float_half),
        ),
        in_specs=[vmem, vmem, hbm, hbm, hbm, vmem, vmem, vmem],
        out_specs=[vmem] * 3,
        scratch_shapes=[
            pltpu.VMEM((feats, width_dp), float_half),
            pltpu.VMEM((table * rank, feats), float_half),
            pltpu.VMEM((table * rank, width), float_half),
            pltpu.VMEM((n_dp * rank, table * rank), jnp.int32),
            pltpu.VMEM((n_dp * rank, both), float_half),
            pltpu.VMEM((n_dp * rank, both), float_half),
            pltpu.VMEM((2 * rank, tok), jnp.float32),
            pltpu.VMEM((n_feat, 2 * rank, tok), jnp.float32),
            pltpu.VMEM((n_dp * rank, both), float_half),
            pltpu.VMEM((n_dp * rank, both), float_half),
            pltpu.VMEM((n_feat, tok // n_feat, width), float_half),
            pltpu.VMEM((n_dp, tok, width_dp), float_half),
            pltpu.VMEM((n_dp, tok, feats), float_half),
            pltpu.VMEM((n_dp + 1, tok, feats), float_half),
            pltpu.VMEM((tok, feats), jnp.float32),
            pltpu.VMEM((tok, feats), jnp.float32),
            dma((3,)),
            *pair,
            *pair,
            *feat_pair,
            *pair,
            *feat_pair,
            *pair,
            dma((n_dp, n_fsdp)),
            dma((n_dp, n_fsdp)),
            dma((n_dp, n_fsdp, n_core)),
            dma((n_dp, n_fsdp, n_core)),
            dma((n_dp,)),
            dma((n_dp + 1,)),
        ],
        compiler_params=pltpu.CompilerParams(
            collective_id=0, has_side_effects=True, vmem_limit_bytes=56 * 2**20
        ),
        cost_estimate=pl.CostEstimate(
            flops=2 * n_dp * tok * width_dp * feats,
            bytes_accessed=2 * (feats * width_dp + 2 * tok * (width + feats)),
            transcendentals=0,
        ),
    )(output_gradient, attention_output, frozen_weight, down, up, asked, key, mask)
    grad_a = lax.dot_general(
        chosen, back[:, :feats], both_major, preferred_element_type=jnp.float32
    ).astype(float_half)
    grad_b = lax.dot_general(
        chosen, back[:, feats:], both_major, preferred_element_type=jnp.float32
    ).astype(float_half)
    grad_a = jnp.transpose(grad_a.reshape(table, rank, feats), (0, 2, 1))
    return input_gradient, grad_a, grad_b.reshape(table, rank, width)


def solution(mesh):
    in_specs = (
        P(("groups", "dp"), ("fsdp", "adapter")),
        P(("groups", "dp"), ("fsdp", "adapter")),
        P(("fsdp", "adapter"), "dp"),
        P(("groups", "dp"), ("fsdp", "adapter"), None),
        P(("groups", "dp"), None, ("fsdp", "adapter")),
        P(("groups", "dp")),
        P(("groups", "dp")),
        P("groups"),
    )
    out_specs = (
        P(("groups", "dp"), ("fsdp", "adapter")),
        P(("groups", "dp"), ("fsdp", "adapter"), None),
        P(("groups", "dp"), None, ("fsdp", "adapter")),
    )
    return jax.shard_map(local, mesh=mesh, in_specs=in_specs, out_specs=out_specs, check_vma=False)
```

```python
import functools

import jax
import jax.numpy as jnp
import numpy as np
from jax import lax
from jax.experimental import pallas as pl
from jax.experimental.pallas import tpu as pltpu
from jax.sharding import PartitionSpec as P

adapter_scale = 2.0
float_half = jnp.bfloat16
both_minor = (((1,), (1,)), ((), ()))
both_major = (((0,), (0,)), ((), ()))


def flip(index, step):
    out, bit = index, 1
    while bit <= step:
        if step & bit:
            out = out + bit - 2 * bit * ((index // bit) % 2)
        bit *= 2
    return out


def copy_to(src, dst, send_sem, recv_sem, device):
    return pltpu.make_async_remote_copy(
        src_ref=src,
        dst_ref=dst,
        send_sem=send_sem,
        recv_sem=recv_sem,
        device_id=device,
        device_id_type=pl.DeviceIdType.MESH,
    )


def kernel(
    n_dp,
    n_fsdp,
    n_core,
    rank,
    waves,
    grad_ref,
    act_ref,
    weight_hbm,
    down_hbm,
    up_hbm,
    key_ref,
    segment_ref,
    first_ref,
    row_ref,
    out_ref,
    back_ref,
    sel_ref,
    weight,
    down,
    up,
    asked_ref,
    asked_in,
    factor_out,
    factor_in,
    proj_out,
    proj_in,
    back_out,
    back_in,
    rows_in,
    grad_all,
    part_out,
    part_in,
    product,
    total,
    load_sem,
    asked_s,
    asked_r,
    factor_s,
    factor_r,
    proj_s,
    proj_r,
    back_s,
    back_r,
    rows_s,
    rows_r,
    grad_s,
    grad_r,
    cross_s,
    cross_r,
    core_s,
    core_r,
    part_s,
    part_r,
):
    dp, fsdp, core = lax.axis_index("dp"), lax.axis_index("fsdp"), lax.axis_index("adapter")
    feat = fsdp * n_core + core
    n_feat = n_fsdp * n_core
    tok, width = grad_ref.shape
    feats = act_ref.shape[1]
    wave_rows = tok // waves
    rows = wave_rows // n_feat
    width_dp = weight.shape[1]
    per_feat = n_dp // n_feat

    def feat_device(index):
        return {"fsdp": index // n_core, "adapter": index % n_core}

    def rank_rows(index):
        return pl.ds(pl.multiple_of(index * rank, rank), rank)

    def token_rows(wave, index):
        return pl.ds(pl.multiple_of(wave * wave_rows + index * rows, rows), rows)

    def wave_slice(wave):
        return pl.ds(wave * wave_rows, wave_rows)

    def share(wave, index, part):
        return grad_all.at[wave, pl.ds(pl.multiple_of(index * wave_rows + part * rows, rows), rows)]

    loads = [
        pltpu.make_async_copy(src, dst, load_sem.at[i])
        for i, (src, dst) in enumerate(((down_hbm, down), (up_hbm, up), (weight_hbm, weight)))
    ]
    for load in loads:
        load.start()

    barrier = pltpu.get_barrier_semaphore()
    for step in range(1, n_dp):
        pl.semaphore_signal(
            barrier,
            inc=1,
            device_id={"dp": flip(dp, step)},
            device_id_type=pl.DeviceIdType.MESH,
        )
    for step in range(1, n_feat):
        pl.semaphore_signal(
            barrier,
            inc=1,
            device_id=feat_device(flip(feat, step)),
            device_id_type=pl.DeviceIdType.MESH,
        )
    pl.semaphore_wait(barrier, n_dp + n_feat - 2)

    def dp_exchange(step, src, dst, send, recv):
        peer = flip(dp, step)
        return copy_to(
            src.at[rank_rows(peer)],
            dst.at[rank_rows(dp)],
            send.at[peer],
            recv.at[dp],
            {"dp": peer},
        )

    def dp_arrival(step, src, dst, send, recv):
        peer = flip(dp, step)
        return copy_to(
            src.at[rank_rows(peer)],
            dst.at[rank_rows(peer)],
            send.at[peer],
            recv.at[peer],
            {"dp": peer},
        )

    asked_args = (asked_ref, asked_in, asked_s, asked_r)
    factor_args = (factor_out, factor_in, factor_s, factor_r)
    back_args = (back_out, back_in, back_s, back_r)

    segs = first_ref.shape[0]
    table = up.shape[0] // rank
    table_rows = [row_ref[segment_ref[seg]] for seg in range(segs)]
    starts = [first_ref[seg] for seg in range(segs)]
    limits = starts[1:] + [tok]
    owned = []
    for owner in range(n_dp):
        wanted, start, limit = 0, 0, 0
        for seg in range(segs):
            local_row = table_rows[seg] - owner * table
            mine = (local_row >= 0) & (local_row < table)
            wanted += jnp.where(mine, local_row + 1, 0)
            start += jnp.where(mine, starts[seg], 0)
            limit += jnp.where(mine, limits[seg], 0)
        owned.append((start, limit))
        asked_ref[owner * rank : (owner + 1) * rank, :] = jnp.full(
            (rank, table * rank), wanted, jnp.int32
        )
    for step in range(1, n_dp):
        dp_exchange(step, *asked_args).start()
    asked_in[rank_rows(dp), :] = asked_ref[rank_rows(dp), :]

    def rows_copy(wave, step):
        peer = flip(feat, step)
        return copy_to(
            grad_ref.at[token_rows(wave, peer)],
            rows_in.at[wave, feat],
            rows_s.at[wave, peer],
            rows_r.at[wave, feat],
            feat_device(peer),
        )

    def rows_arrival(wave, step):
        peer = flip(feat, step)
        return copy_to(
            grad_ref.at[token_rows(wave, peer)],
            rows_in.at[wave, peer],
            rows_s.at[wave, peer],
            rows_r.at[wave, peer],
            feat_device(peer),
        )

    def spread_rows(wave):
        for step in range(1, n_feat):
            rows_copy(wave, step).start()

    def grad_copy(wave, step, part):
        source = flip(feat, step)
        target = source * per_feat + part
        columns = pl.ds(part * width_dp, width_dp)
        if step == 0:
            block = grad_ref.at[token_rows(wave, feat), columns]
        else:
            block = rows_in.at[wave, source, :, columns]
        copy = copy_to(
            block,
            share(wave, dp, feat),
            grad_s.at[wave, target],
            grad_r.at[wave, dp],
            {"dp": target},
        )
        return target, block, copy

    def forward(wave, step):
        for part in range(per_feat):
            target, block, copy = grad_copy(wave, step, part)

            @pl.when(target != dp)
            def _():
                copy.start()

            @pl.when(target == dp)
            def _():
                share(wave, dp, feat)[...] = block[...]

    spread_rows(0)
    forward(0, 0)

    def factors():
        loads[0].wait()
        loads[1].wait()
        for step in range(1, n_dp):
            dp_arrival(step, *asked_args).wait_recv()
        chosen = jnp.where(asked_in[...] - 1 == key_ref[...], 1.0, 0.0).astype(float_half)
        sel_ref[...] = chosen
        factor_out[:, :feats] = jnp.dot(
            chosen, down[...], preferred_element_type=jnp.float32
        ).astype(float_half)
        factor_out[:, feats:] = jnp.dot(
            chosen, up[...], preferred_element_type=jnp.float32
        ).astype(float_half)
        for step in range(1, n_dp):
            dp_exchange(step, *factor_args).start()
        factor_in[rank_rows(dp), :] = factor_out[rank_rows(dp), :]

    def proj_copy(step):
        peer = flip(feat, step)
        return copy_to(
            proj_out, proj_in.at[feat], proj_s.at[peer], proj_r.at[feat], feat_device(peer)
        )

    def proj_arrival(step):
        peer = flip(feat, step)
        return copy_to(
            proj_out, proj_in.at[peer], proj_s.at[peer], proj_r.at[peer], feat_device(peer)
        )

    def in_owner(owner):
        places = lax.broadcasted_iota(jnp.int32, (rank, tok), 1)
        start, limit = owned[owner]
        return (places >= start) & (places < limit)

    def project():
        for step in range(1, n_dp):
            dp_arrival(step, *factor_args).wait_recv()
        for half, (factor, value) in enumerate(
            ((factor_in[:, feats:], grad_ref[...]), (factor_in[:, :feats], act_ref[...]))
        ):
            product = lax.dot_general(
                factor, value, both_minor, preferred_element_type=jnp.float32
            )
            folded = jnp.zeros((rank, tok), jnp.float32)
            for owner in range(n_dp):
                folded += jnp.where(
                    in_owner(owner), product[owner * rank : (owner + 1) * rank], 0.0
                )
            proj_out[half * rank : (half + 1) * rank, :] = folded
        for step in range(1, n_feat):
            proj_copy(step).start()
        proj_in[feat] = proj_out[...]

    def adapter_gradients():
        for step in range(1, n_feat):
            proj_arrival(step).wait_recv()
        summed = proj_in[0]
        for index in range(1, n_feat):
            summed += proj_in[index]

        def spread(values):
            return jnp.concatenate(
                [jnp.where(in_owner(owner), values, 0.0) for owner in range(n_dp)], axis=0
            ).astype(float_half)

        up_block, down_block = spread(summed[:rank]), spread(summed[rank:])
        back_out[:, :feats] = (
            adapter_scale
            * jnp.dot(up_block, act_ref[...], preferred_element_type=jnp.float32)
        ).astype(float_half)
        back_out[:, feats:] = (
            adapter_scale
            * jnp.dot(down_block, grad_ref[...], preferred_element_type=jnp.float32)
        ).astype(float_half)
        for step in range(1, n_dp):
            dp_exchange(step, *back_args).start()
        back_in[rank_rows(dp), :] = back_out[rank_rows(dp), :]
        total[...] += adapter_scale * lax.dot_general(
            up_block, factor_in[:, :feats], both_major, preferred_element_type=jnp.float32
        )

    def grad_arrival(wave, peer):
        block = share(wave, peer, feat)
        return copy_to(block, block, grad_s.at[wave, peer], grad_r.at[wave, peer], {"dp": peer})

    def cross_copy(wave, index, step):
        peer = flip(fsdp, step)
        block = share(wave, index, feat)
        return copy_to(
            block,
            block,
            cross_s.at[wave, index, peer],
            cross_r.at[wave, index, fsdp],
            {"fsdp": peer},
        )

    def cross_arrival(wave, index, step):
        peer = flip(fsdp, step)
        block = share(wave, index, peer * n_core + core)
        return copy_to(
            block,
            block,
            cross_s.at[wave, index, peer],
            cross_r.at[wave, index, peer],
            {"fsdp": peer},
        )

    def core_copy(wave, index, step, side):
        chip, peer = flip(fsdp, step), flip(core, side)
        block = share(wave, index, chip * n_core + core)
        return copy_to(
            block,
            block,
            core_s.at[wave, index, chip, peer],
            core_r.at[wave, index, chip, core],
            {"adapter": peer},
        )

    def core_arrival(wave, index, step, side):
        chip, peer = flip(fsdp, step), flip(core, side)
        block = share(wave, index, chip * n_core + peer)
        return copy_to(
            block,
            block,
            core_s.at[wave, index, chip, peer],
            core_r.at[wave, index, chip, peer],
            {"adapter": peer},
        )

    def order(turn):
        if turn == 0:
            return dp
        upper = dp // (n_dp // 2)
        falling, rising = n_dp - turn, turn - 1
        falling = falling - (dp - falling + n_dp) // n_dp
        rising = rising + (rising - dp + n_dp) // n_dp
        return (1 - upper) * falling + upper * rising

    def part_copy(wave, turn):
        index = order(turn)
        above = (index - dp - 1 + n_dp) // n_dp
        following = dp + 2 * above - 1
        ends = (1 - above) * (1 - (following - index + n_dp - 1) // n_dp)
        slot = index + ends * (n_dp - index)
        return copy_to(
            part_out.at[wave, index],
            part_in.at[wave, slot],
            part_s.at[wave, index],
            part_r.at[wave, slot],
            {"dp": following},
        )

    def part_arrival(wave, slot):
        return copy_to(
            part_out.at[wave, 0],
            part_in.at[wave, slot],
            part_s.at[wave, 0],
            part_r.at[wave, slot],
            {"dp": flip(dp, 1)},
        )

    tile = 256 if feats % 256 == 0 else feats
    outermost = dp * (n_dp - 1 - dp) == 0

    def rows_of(index):
        return pl.ds(pl.multiple_of(index * wave_rows, wave_rows), wave_rows)

    def forward_all(wave):
        if wave + 1 < waves:
            spread_rows(wave + 1)
        if wave:
            forward(wave, 0)
        for step in range(1, n_feat):
            rows_arrival(wave, step).wait_recv()
            forward(wave, step)

    def collect(wave):
        for turn in range(n_dp):
            index = order(turn)
            if turn:
                grad_arrival(wave, index).wait_recv()
            for step in range(1, n_fsdp):
                cross_copy(wave, index, step).start()
            for side in range(1, n_core):
                core_copy(wave, index, 0, side).start()

    def hand_over(wave):
        for turn in range(n_dp):
            index = order(turn)
            for step in range(1, n_fsdp):
                cross_arrival(wave, index, step).wait_recv()
                for side in range(1, n_core):
                    core_copy(wave, index, step, side).start()

    def multiply(wave):
        for turn in range(n_dp):
            for step in range(n_fsdp):
                for side in range(1, n_core):
                    core_arrival(wave, order(turn), step, side).wait_recv()

        def one(i, carry):
            columns = pl.ds(pl.multiple_of(i * tile, tile), tile)
            product[:, columns] = lax.dot_general(
                grad_all[wave], weight[columns, :], both_minor, preferred_element_type=jnp.float32
            )
            return carry

        lax.fori_loop(0, feats // tile, one, 0)

        @pl.when(outermost)
        def _():
            for turn in range(1, n_dp):
                index = order(turn)
                part_out[wave, index] = product[rows_of(index), :].astype(float_half)
                part_copy(wave, turn).start()

        total[wave_slice(wave), :] += product[rows_of(dp), :]

    def chain(wave):
        @pl.when(jnp.logical_not(outermost))
        def _():
            for turn in range(1, n_dp):
                index = order(turn)
                part_arrival(wave, index).wait_recv()
                part_out[wave, index] = (
                    product[rows_of(index), :] + part_in[wave, index].astype(jnp.float32)
                ).astype(float_half)
                part_copy(wave, turn).start()

    total[...] = jnp.zeros_like(total)
    forward_all(0)
    for wave in range(1, waves + 3):
        if wave < waves:
            forward_all(wave)
        if wave == 1:
            factors()
        if 0 <= wave - 1 < waves:
            collect(wave - 1)
        if wave == 2:
            project()
            loads[2].wait()
        if 0 <= wave - 2 < waves:
            hand_over(wave - 2)
        if 0 <= wave - 3 < waves:
            chain(wave - 3)
        if 0 <= wave - 2 < waves:
            multiply(wave - 2)
        if wave == 3:
            adapter_gradients()

    for wave in range(waves):
        for slot, there in ((dp, dp > 0), (n_dp, dp < n_dp - 1)):

            @pl.when(there)
            def _():
                part_arrival(wave, slot).wait_recv()
                total[wave_slice(wave), :] += part_in[wave, slot].astype(jnp.float32)

    out_ref[...] = total[...].astype(float_half)
    for step in range(1, n_dp):
        dp_arrival(step, *back_args).wait_recv()
    back_ref[...] = back_in[...]

    for step in range(1, n_dp):
        for args in (asked_args, factor_args, back_args):
            dp_exchange(step, *args).wait_send()
    for step in range(1, n_feat):
        proj_copy(step).wait_send()
    for wave in range(waves):
        for step in range(1, n_dp):
            part_copy(wave, step).wait_send()
        for step in range(1, n_feat):
            rows_copy(wave, step).wait_send()
        for step in range(n_feat):
            for part in range(per_feat):
                target, _, copy = grad_copy(wave, step, part)

                @pl.when(target != dp)
                def _():
                    copy.wait_send()

        for turn in range(n_dp):
            index = flip(dp, turn)
            for step in range(1, n_fsdp):
                cross_copy(wave, index, step).wait_send()
            for step in range(n_fsdp):
                for side in range(1, n_core):
                    core_copy(wave, index, step, side).wait_send()


def place(chosen_ref, back_ref, in_ref, a_ref, b_ref, out_ref):
    feats = a_ref.shape[1]
    a_ref[...] = lax.dot_general(
        chosen_ref[...], back_ref[:, :feats], both_major, preferred_element_type=jnp.float32
    ).astype(float_half)
    b_ref[...] = lax.dot_general(
        chosen_ref[...], back_ref[:, feats:], both_major, preferred_element_type=jnp.float32
    ).astype(float_half)
    out_ref[...] = in_ref[...]


def local(
    output_gradient,
    attention_output,
    frozen_weight,
    adapter_down_table,
    adapter_up_table,
    segment_adapter,
    segment_first_token,
    adapter_table_row,
):
    n_dp, n_fsdp, n_core = (lax.axis_size(name) for name in ("dp", "fsdp", "adapter"))
    n_feat = n_fsdp * n_core
    tok, width = output_gradient.shape
    table, feats, rank = adapter_down_table.shape
    width_dp = frozen_weight.shape[1]
    row_of = np.arange(n_dp * rank, dtype=np.int32)[:, None]
    col_of = np.arange(table * rank, dtype=np.int32)[None, :]
    key = jnp.asarray(
        np.where(row_of % rank == col_of % rank, col_of // rank, -5).astype(np.int32)
    )
    down = jnp.transpose(adapter_down_table, (0, 2, 1)).reshape(table * rank, feats)
    up = adapter_up_table.reshape(table * rank, width)
    both = feats + width
    waves = 3 if tok % (3 * 16 * n_feat) == 0 else 1
    vmem = pl.BlockSpec(memory_space=pltpu.VMEM)
    hbm = pl.BlockSpec(memory_space=pl.ANY)
    smem = pl.BlockSpec(memory_space=pltpu.SMEM)
    dma = pltpu.SemaphoreType.DMA
    pair = [dma((n_dp,)), dma((n_dp,))]
    feat_pair = [dma((n_feat,)), dma((n_feat,))]
    input_gradient, back, chosen = pl.pallas_call(
        functools.partial(kernel, n_dp, n_fsdp, n_core, rank, waves),
        out_shape=(
            jax.ShapeDtypeStruct((tok, feats), float_half),
            jax.ShapeDtypeStruct((n_dp * rank, both), float_half),
            jax.ShapeDtypeStruct((n_dp * rank, table * rank), float_half),
        ),
        in_specs=[vmem, vmem, hbm, hbm, hbm, vmem, smem, smem, smem],
        out_specs=[vmem] * 3,
        scratch_shapes=[
            pltpu.VMEM((feats, width_dp), float_half),
            pltpu.VMEM((table * rank, feats), float_half),
            pltpu.VMEM((table * rank, width), float_half),
            pltpu.VMEM((n_dp * rank, table * rank), jnp.int32),
            pltpu.VMEM((n_dp * rank, table * rank), jnp.int32),
            pltpu.VMEM((n_dp * rank, both), float_half),
            pltpu.VMEM((n_dp * rank, both), float_half),
            pltpu.VMEM((2 * rank, tok), jnp.float32),
            pltpu.VMEM((n_feat, 2 * rank, tok), jnp.float32),
            pltpu.VMEM((n_dp * rank, both), float_half),
            pltpu.VMEM((n_dp * rank, both), float_half),
            pltpu.VMEM((waves, n_feat, tok // waves // n_feat, width), float_half),
            pltpu.VMEM((waves, n_dp * tok // waves, width_dp), float_half),
            pltpu.VMEM((waves, n_dp, tok // waves, feats), float_half),
            pltpu.VMEM((waves, n_dp + 1, tok // waves, feats), float_half),
            pltpu.VMEM((n_dp * tok // waves, feats), jnp.float32),
            pltpu.VMEM((tok, feats), jnp.float32),
            dma((3,)),
            *pair,
            *pair,
            *feat_pair,
            *pair,
            dma((waves, n_feat)),
            dma((waves, n_feat)),
            dma((waves, n_dp)),
            dma((waves, n_dp)),
            dma((waves, n_dp, n_fsdp)),
            dma((waves, n_dp, n_fsdp)),
            dma((waves, n_dp, n_fsdp, n_core)),
            dma((waves, n_dp, n_fsdp, n_core)),
            dma((waves, n_dp)),
            dma((waves, n_dp + 1)),
        ],
        compiler_params=pltpu.CompilerParams(
            collective_id=0, has_side_effects=True, vmem_limit_bytes=56 * 2**20
        ),
        cost_estimate=pl.CostEstimate(
            flops=2 * n_dp * tok * width_dp * feats,
            bytes_accessed=2 * (feats * width_dp + 2 * tok * (width + feats)),
            transcendentals=0,
        ),
    )(
        output_gradient,
        attention_output,
        frozen_weight,
        down,
        up,
        key,
        segment_adapter,
        segment_first_token,
        adapter_table_row,
    )
    steps = 4
    slots, tokens = table * rank // steps, tok // steps
    grad_a, grad_b, input_gradient = pl.pallas_call(
        place,
        grid=(steps,),
        out_shape=(
            jax.ShapeDtypeStruct((table * rank, feats), float_half),
            jax.ShapeDtypeStruct((table * rank, width), float_half),
            jax.ShapeDtypeStruct((tok, feats), float_half),
        ),
        in_specs=[
            pl.BlockSpec((n_dp * rank, slots), lambda i: (0, i)),
            pl.BlockSpec((n_dp * rank, both), lambda i: (0, 0)),
            pl.BlockSpec((tokens, feats), lambda i: (i, 0)),
        ],
        out_specs=[
            pl.BlockSpec((slots, feats), lambda i: (i, 0)),
            pl.BlockSpec((slots, width), lambda i: (i, 0)),
            pl.BlockSpec((tokens, feats), lambda i: (i, 0)),
        ],
        compiler_params=pltpu.CompilerParams(vmem_limit_bytes=32 * 2**20),
    )(chosen, back, input_gradient)
    grad_a = jnp.transpose(grad_a.reshape(table, rank, feats), (0, 2, 1))
    return input_gradient, grad_a, grad_b.reshape(table, rank, width)


def solution(mesh):
    in_specs = (
        P(("groups", "dp"), ("fsdp", "adapter")),
        P(("groups", "dp"), ("fsdp", "adapter")),
        P(("fsdp", "adapter"), "dp"),
        P(("groups", "dp"), ("fsdp", "adapter"), None),
        P(("groups", "dp"), None, ("fsdp", "adapter")),
        P(("groups", "dp")),
        P(("groups", "dp")),
        P("groups"),
    )
    out_specs = (
        P(("groups", "dp"), ("fsdp", "adapter")),
        P(("groups", "dp"), ("fsdp", "adapter"), None),
        P(("groups", "dp"), None, ("fsdp", "adapter")),
    )
    return jax.shard_map(local, mesh=mesh, in_specs=in_specs, out_specs=out_specs, check_vma=False)
```
